32 devices in a mesh: group: 2 (over y), space: 8 (over z, x), tm: 2 (over core).
Axes of the slice: x: 2, y: 2, z: 4, core: 2. Of those that a mesh axis runs over, the one named last changes fastest.
Arguments:
- snapshots: bfloat16 [2048, 8192], P(('group', 'tm'), 'space'), parts along dimension 0, may hold values from -6 to 6
- mode_columns: bfloat16 [8192, 96], P('space', 'group'), parts along dimension 1, may hold values from -0.0625 to 0.0625
- filter_taps: bfloat16 [8, 2, 257], replicated, may hold values from -1 to 1, as said below
- mode_gain: float32 [96], P('group'), parts along dimension 0, may hold values from 2 to 20
Outputs:
- band_field: bfloat16 [2048, 8192], P(('group', 'tm'), 'space'), parts along dimension 0
The draws below stay inside these ranges and needn't reach their ends.
There are 2 independent parts, one for each index of `group`. The reference program is written for one: setup_inputs(seed, part) draws one part's arguments, and reference() takes and returns one part's arrays. A program takes and returns all parts, laid end to end along the dimension named above; an argument that names none is the same for every part. Nothing has to cross between parts.
Inputs may be any that keep to these rules, and one draw needn't show every extreme that they name: `filter_taps`: each frequency's taps are a tapered cosine and sine of some frequency, each tap then scaled by an independent factor between 0.5 and 1.5.
All inputs are finite; a program needn't handle non-finite values.
Results may differ from the reference program's by a relative error of at most 0.0059.
Values may be sent and summed in bfloat16 or wider, within the bound.
No kernel may reach another device: no remote copies, remote signals or barrier semaphores. Data moves between devices by JAX's collectives and lax.ppermute only.
A program may use at most 64 MiB of HBM per device.

```python
import math
import jax
import jax.numpy as jnp
from jax import lax

HALF = 128
TAPS = 257
NDOF = 8192
NF = 8
M = 48
NT = 1024


def draw_filter_taps(key, part):
    key = jax.random.fold_in(key, 7)
    key_omega, key_jitter = jax.random.split(key)
    omega = jax.random.uniform(key_omega, (NF, 1), jnp.float32, 0.05, 2.5)
    offset = jnp.arange(TAPS, dtype=jnp.float32) - HALF
    taper = 0.5 - 0.5 * jnp.cos(2.0 * jnp.pi * (offset + HALF + 1.0) / (TAPS + 1.0))
    factor = jnp.sqrt(16.0 / (3.0 * TAPS))
    jitter = jax.random.uniform(key_jitter, (NF, 2, TAPS), jnp.float32, 0.5, 1.5)
    cosine = taper * jnp.cos(omega * offset) * factor
    sine = taper * jnp.sin(omega * offset) * factor
    return (jnp.stack([cosine, sine], axis=1) * jitter).astype(jnp.bfloat16)


def steps_of(own_key, shape, cuts, low, largest):
    gain = 1.0
    for axis_at, blocks in cuts:
        draws = jax.random.uniform(jax.random.fold_in(jax.random.fold_in(own_key, 6), axis_at), (blocks,), jnp.float32, low / len(cuts), largest / len(cuts))
        gain = gain * jnp.repeat(jnp.exp(draws), shape[axis_at] // blocks).reshape((-1,) + (1,) * (len(shape) - 1 - axis_at))
    return gain


def gaussian(key, extent, width, bound, pieces=(), held_as=jnp.bfloat16):
    values = jax.random.normal(key, extent, jnp.float32) * width
    if len(pieces) > 0:
        values = steps_of(key, extent, pieces, -0.22, 0.18) * values
    return jnp.clip(values, min=-bound, max=bound).astype(held_as)


def setup_inputs(seed: int = 0, part: int = 0) -> dict:
    arg_keys = jax.random.split(jax.random.key(seed), 5)
    part_splits = jax.random.split(jax.random.fold_in(arg_keys[4], part), 5)
    snapshots = gaussian(part_splits[0], (NT, NDOF), 1.0, 6.0, ((0, 2), (1, 8)))
    mode_columns = gaussian(part_splits[1], (NDOF, M), NDOF ** -0.5, 0.0625, ((0, 8),))
    filter_taps = draw_filter_taps(jax.random.fold_in(arg_keys[4], 71), part)
    mode_gain = jnp.clip(jnp.exp(jax.random.uniform(part_splits[3], (M,), jnp.float32, math.log(2.0), math.log(20.0))), 2.0, 20.0)
    return dict(snapshots=snapshots, mode_columns=mode_columns, filter_taps=filter_taps, mode_gain=mode_gain)


def band_filter(coefficients, filter_taps):
    freqs = filter_taps.shape[0]
    modes = coefficients.shape[0] // (2 * freqs)
    padlen = coefficients.shape[1]
    stacked = coefficients.reshape(freqs, modes, 2, padlen).transpose(1, 0, 2, 3).reshape(modes, freqs * 2, padlen)
    cosine = filter_taps[:, 0, :]
    sine = filter_taps[:, 1, :]
    row_cos = jnp.stack([cosine, -sine], axis=1)
    row_sin = jnp.stack([sine, cosine], axis=1)
    kernel = jnp.stack([row_cos, row_sin], axis=1).reshape(freqs * 2, 2, filter_taps.shape[2])
    result = lax.conv_general_dilated(stacked, kernel, (1,), "VALID", feature_group_count=freqs, dimension_numbers=("NCH", "OIH", "NCH"), preferred_element_type=jnp.float32)
    steps = result.shape[2]
    return result.reshape(modes, freqs, 2, steps).transpose(1, 0, 2, 3).reshape(freqs * modes * 2, steps)


def reference(snapshots, mode_columns, filter_taps, mode_gain):
    coeffs = lax.dot_general(mode_columns, snapshots, (((0,), (1,)), ((), ())), preferred_element_type=jnp.float32)
    rounded = coeffs.astype(jnp.bfloat16)
    padded = jnp.pad(rounded, ((0, 0), (HALF, HALF)))
    filtered = band_filter(padded, filter_taps)
    scaled = (filtered * mode_gain[:, None]).astype(jnp.bfloat16)
    field = lax.dot_general(scaled, mode_columns, (((0,), (1,)), ((), ())), preferred_element_type=jnp.float32)
    return field.astype(jnp.bfloat16)
```

```python
import functools

import jax
import jax.numpy as jnp
from jax import lax
from jax.experimental import pallas as pl
from jax.experimental.pallas import tpu as pltpu
from jax.sharding import PartitionSpec as P

HALF = 128
WINDOW = 3 * HALF
CHUNK = 8
LAST = (((1,), (1,)), ((), ()))
FIRST = (((0,), (0,)), ((), ()))


def coefficient_kernel(columns_hbm, snapshots_hbm, out_ref, columns, snapshots, sems):
    steps = snapshots.shape[0]
    pieces = steps // HALF
    head = pltpu.make_async_copy(columns_hbm, columns, sems.at[pieces])
    copies = [
        pltpu.make_async_copy(
            snapshots_hbm.at[pl.ds(i * HALF, HALF)], snapshots.at[pl.ds(i * HALF, HALF)], sems.at[i]
        )
        for i in range(pieces)
    ]
    head.start()
    for copy in copies:
        copy.start()
    head.wait()
    for i, copy in enumerate(copies):
        copy.wait()
        span = slice(i * HALF, (i + 1) * HALF)
        out_ref[:, span] = lax.dot_general(
            columns[...], snapshots[span, :], LAST, preferred_element_type=jnp.float32
        )


def coefficients(columns, snapshots):
    rows, dofs = columns.shape
    steps = snapshots.shape[0]
    return pl.pallas_call(
        coefficient_kernel,
        out_shape=jax.ShapeDtypeStruct((rows, steps), jnp.float32),
        in_specs=[pl.BlockSpec(memory_space=pl.ANY)] * 2,
        out_specs=pl.BlockSpec(memory_space=pltpu.VMEM),
        scratch_shapes=[
            pltpu.VMEM((rows, dofs), jnp.bfloat16),
            pltpu.VMEM((steps, dofs), jnp.bfloat16),
            pltpu.SemaphoreType.DMA((steps // HALF + 1,)),
        ],
        compiler_params=pltpu.CompilerParams(vmem_limit_bytes=16 << 20),
        cost_estimate=pl.CostEstimate(
            flops=2 * rows * dofs * steps, bytes_accessed=2 * steps * dofs, transcendentals=0
        ),
        name="coefficients",
    )(columns, snapshots)


def band_kernel(taps_ref, out_ref):
    for f in range(out_ref.shape[0]):
        for part in range(2):
            row = taps_ref[2 * f + part : 2 * f + part + 1, :]
            square = jnp.broadcast_to(row, (HALF, WINDOW))
            out_ref[f, :, part * WINDOW : (part + 1) * WINDOW] = pltpu.roll(
                square, 0, 1, stride=1, stride_axis=0
            ).astype(jnp.bfloat16)


def band_matrices(filter_taps):
    freqs, parts, taps = filter_taps.shape
    padded = jnp.pad(
        filter_taps.astype(jnp.float32).reshape(freqs * parts, taps), ((0, 0), (0, WINDOW - taps))
    )
    chunk = min(CHUNK, freqs)
    return pl.pallas_call(
        band_kernel,
        grid=(freqs // chunk,),
        out_shape=jax.ShapeDtypeStruct((freqs, HALF, 2 * WINDOW), jnp.bfloat16),
        in_specs=[pl.BlockSpec((2 * chunk, WINDOW), lambda i: (i, 0))],
        out_specs=pl.BlockSpec((chunk, HALF, 2 * WINDOW), lambda i: (i, 0, 0)),
        compiler_params=pltpu.CompilerParams(vmem_limit_bytes=16 << 20),
        cost_estimate=pl.CostEstimate(
            flops=freqs * HALF * WINDOW * 40, bytes_accessed=freqs * HALF * WINDOW * 4, transcendentals=0
        ),
        name="band_matrices",
    )(padded)


def field_kernel(
    chunks, coeffs_ref, halo_ref, bands_ref, gain_ref, columns_ref, out_hbm, wide, scaled, field, total, sems
):
    rows, steps = coeffs_ref.shape
    blocks = steps // HALF
    freqs = bands_ref.shape[0]
    modes = rows // freqs
    after = lax.axis_index("tm") == 0
    halo = halo_ref[...].astype(jnp.float32)
    none = jnp.zeros_like(halo)
    cells = jnp.concatenate(
        [
            jnp.where(after, none, halo),
            coeffs_ref[...].astype(jnp.bfloat16).astype(jnp.float32),
            jnp.where(after, halo, none),
        ],
        axis=1,
    )
    cosine = lax.broadcasted_iota(jnp.int32, cells.shape, 0) % 2 == 0
    turned = jnp.where(cosine, -pltpu.roll(cells, rows - 1, 0), pltpu.roll(cells, 1, 0))
    wide[0, :rows, :] = cells
    wide[1, :rows, :] = turned
    wide[:, rows:, :] = jnp.zeros((2, 8, cells.shape[1]), jnp.float32)
    for f in range(freqs):
        at = f * modes
        own = wide[0, at : at + 8, :]
        other = wide[1, at : at + 8, :]
        inputs = jnp.concatenate(
            [
                jnp.concatenate(
                    [own[:, b * HALF : b * HALF + WINDOW], other[:, b * HALF : b * HALF + WINDOW]], axis=1
                )
                for b in range(blocks)
            ],
            axis=0,
        ).astype(jnp.bfloat16)
        filtered = lax.dot_general(inputs, bands_ref[f], LAST, preferred_element_type=jnp.float32)
        for b in range(blocks):
            scaled[at : at + 8, b * HALF : (b + 1) * HALF] = filtered[8 * b : 8 * b + 8]
    step = pl.program_id(0)
    columns = columns_ref[...]
    copies = []
    for b in range(blocks):
        span = slice(b * HALF, (b + 1) * HALF)
        piece = (scaled[:rows, span] * gain_ref[...]).astype(jnp.bfloat16)
        part = lax.dot_general(piece, columns, FIRST, preferred_element_type=jnp.float32)
        copy = pltpu.make_async_copy(field.at[pl.ds(b * HALF, HALF)], out_hbm.at[pl.ds(b * HALF, HALF)], sems.at[b])
        if chunks == 1:
            field[span, :] = part.astype(jnp.bfloat16)
            copy.start()
            copies.append(copy)
        else:

            @pl.when(step == 0)
            def _():
                total[span, :] = part

            @pl.when(step > 0)
            def _():
                total[span, :] += part

            @pl.when(step == chunks - 1)
            def _():
                field[span, :] = total[span, :].astype(jnp.bfloat16)
                copy.start()
                copy.wait()

    for copy in copies:
        copy.wait()


def band_field(coeffs, halo, bands, gain, columns):
    rows, steps = coeffs.shape
    dofs = columns.shape[1]
    freqs = bands.shape[0]
    chunk = min(CHUNK, freqs)
    chunks = freqs // chunk
    held = rows // chunks
    return pl.pallas_call(
        functools.partial(field_kernel, chunks),
        grid=(chunks,),
        out_shape=jax.ShapeDtypeStruct((steps, dofs), jnp.bfloat16),
        in_specs=[
            pl.BlockSpec((held, steps), lambda i: (i, 0)),
            pl.BlockSpec((held, HALF), lambda i: (i, 0)),
            pl.BlockSpec((chunk, HALF, 2 * WINDOW), lambda i: (i, 0, 0)),
            pl.BlockSpec((held, HALF), lambda i: (i, 0)),
            pl.BlockSpec((held, dofs), lambda i: (i, 0)),
        ],
        out_specs=pl.BlockSpec(memory_space=pl.ANY),
        scratch_shapes=[
            pltpu.VMEM((2, held + 8, steps + 2 * HALF), jnp.float32),
            pltpu.VMEM((held + 8, steps), jnp.float32),
            pltpu.VMEM((steps, dofs), jnp.bfloat16),
            pltpu.VMEM((steps if chunks > 1 else 8, dofs), jnp.float32),
            pltpu.SemaphoreType.DMA((steps // HALF,)),
        ],
        compiler_params=pltpu.CompilerParams(vmem_limit_bytes=32 << 20),
        cost_estimate=pl.CostEstimate(
            flops=2 * rows * dofs * steps, bytes_accessed=2 * steps * dofs, transcendentals=0
        ),
        name="band_field",
    )(coeffs, halo, bands, gain, columns)


def summed(values, axis):
    count = lax.axis_size(axis)
    apart = 1
    while apart < count:
        values = values + lax.ppermute(values, axis, [(i, i ^ apart) for i in range(count)])
        apart *= 2
    return values


def per_device(snapshots, mode_columns, filter_taps, mode_gain):
    columns = mode_columns.T
    gain = jnp.broadcast_to(mode_gain[:, None], (mode_gain.shape[0], HALF))
    bands = band_matrices(filter_taps)
    coeffs = summed(coefficients(columns, snapshots), "space")
    edge = jnp.where(lax.axis_index("tm") == 0, coeffs[:, -HALF:], coeffs[:, :HALF])
    halo = lax.ppermute(edge.astype(jnp.bfloat16), "tm", [(0, 1), (1, 0)])
    return band_field(coeffs, halo, bands, gain, columns)


def solution(mesh):
    placed = (P(("group", "tm"), "space"), P("space", "group"), P(), P("group"))
    return jax.shard_map(
        per_device,
        mesh=mesh,
        in_specs=placed,
        out_specs=P(("group", "tm"), "space"),
        check_vma=False,
    )
```

```python
import functools
import math

import jax
import jax.numpy as jnp
from jax import lax
from jax.experimental import pallas as pl
from jax.experimental.pallas import tpu as pltpu
from jax.sharding import PartitionSpec as P

HALF = 128
WINDOW = 3 * HALF
CHUNK = 8
SPLITS = 4
LAST = (((1,), (1,)), ((), ()))
FIRST = (((0,), (0,)), ((), ()))
WHOLE = pl.BlockSpec(memory_space=pltpu.VMEM)


def coefficient_kernel(columns_hbm, snapshots_hbm, out_ref, columns, snapshots, sems):
    width = snapshots.shape[1] // SPLITS
    head = pltpu.make_async_copy(columns_hbm, columns, sems.at[SPLITS])
    head.start()
    copies = []
    for i in range(SPLITS):
        span = pl.ds(i * width, width)
        copies.append(pltpu.make_async_copy(snapshots_hbm.at[:, span], snapshots.at[:, span], sems.at[i]))
        copies[-1].start()
    head.wait()
    total = None
    for i, copy in enumerate(copies):
        copy.wait()
        span = slice(i * width, (i + 1) * width)
        part = lax.dot_general(columns[:, span], snapshots[:, span], LAST, preferred_element_type=jnp.float32)
        total = part if total is None else total + part
    out_ref[...] = total


def coefficients(columns, snapshots):
    rows, dofs = columns.shape
    steps = snapshots.shape[0]
    return pl.pallas_call(
        coefficient_kernel,
        out_shape=pltpu.VMEM((rows, steps), jnp.float32),
        in_specs=[pl.BlockSpec(memory_space=pltpu.HBM)] * 2,
        out_specs=WHOLE,
        scratch_shapes=[
            pltpu.VMEM((rows, dofs), jnp.bfloat16),
            pltpu.VMEM((steps, dofs), jnp.bfloat16),
            pltpu.SemaphoreType.DMA((SPLITS + 1,)),
        ],
        compiler_params=pltpu.CompilerParams(vmem_limit_bytes=16 << 20),
        cost_estimate=pl.CostEstimate(
            flops=2 * rows * dofs * steps, bytes_accessed=2 * steps * dofs, transcendentals=0
        ),
        name="coefficients",
    )(pltpu.with_memory_space_constraint(columns, pltpu.HBM), pltpu.with_memory_space_constraint(snapshots, pltpu.HBM))


def band_kernel(taps_ref, out_ref):
    for f in range(out_ref.shape[0]):
        for part in range(2):
            row = taps_ref[2 * f + part : 2 * f + part + 1, :]
            square = jnp.broadcast_to(row, (HALF, WINDOW))
            out_ref[f, :, part * WINDOW : (part + 1) * WINDOW] = pltpu.roll(
                square, 0, 1, stride=1, stride_axis=0
            ).astype(jnp.bfloat16)


def padded_taps(filter_taps):
    freqs, parts, taps = filter_taps.shape
    rows = filter_taps.astype(jnp.float32).reshape(freqs * parts, taps)
    return jnp.pad(rows, ((0, 0), (0, WINDOW - taps)))


def band_matrices(taps):
    freqs = taps.shape[0] // 2
    chunk = min(CHUNK, freqs)
    one = freqs == chunk
    shape = (freqs, HALF, 2 * WINDOW)
    return pl.pallas_call(
        band_kernel,
        grid=() if one else (freqs // chunk,),
        out_shape=pltpu.VMEM(shape, jnp.bfloat16) if one else jax.ShapeDtypeStruct(shape, jnp.bfloat16),
        in_specs=[WHOLE if one else pl.BlockSpec((2 * chunk, WINDOW), lambda i: (i, 0))],
        out_specs=WHOLE if one else pl.BlockSpec((chunk, HALF, 2 * WINDOW), lambda i: (i, 0, 0)),
        compiler_params=pltpu.CompilerParams(vmem_limit_bytes=16 << 20),
        cost_estimate=pl.CostEstimate(
            flops=freqs * HALF * WINDOW * 40, bytes_accessed=freqs * HALF * WINDOW * 4, transcendentals=0
        ),
        name="band_matrices",
    )(taps)


def turned(cells):
    cosine = lax.broadcasted_iota(jnp.int32, cells.shape, 0) % 2 == 0
    return jnp.where(cosine, -pltpu.roll(cells, cells.shape[0] - 1, 0), pltpu.roll(cells, 1, 0))


def add_over_chunks(chunks, total, span, part, store):
    if chunks == 1:
        store(part)
        return
    step = pl.program_id(0)
    total[span, :] = jnp.where(step == 0, part, total[span, :] + part)

    @pl.when(step == chunks - 1)
    def _():
        store(total[span, :])


def own_kernel(chunks, coeffs_ref, bands_ref, gain_ref, columns_ref, filtered_ref, field_ref, wide, total):
    rows, steps = coeffs_ref.shape
    blocks = steps // HALF
    freqs = bands_ref.shape[0]
    modes = rows // freqs
    cells = coeffs_ref[...].astype(jnp.bfloat16).astype(jnp.float32)
    for i, part in enumerate((cells, turned(cells))):
        wide[i, :, :HALF] = jnp.zeros((rows + 8, HALF), jnp.float32)
        wide[i, :, HALF + steps :] = jnp.zeros((rows + 8, HALF), jnp.float32)
        wide[i, :rows, HALF : HALF + steps] = part
        wide[i, rows:, HALF : HALF + steps] = jnp.zeros((8, steps), jnp.float32)
    for f in range(freqs):
        at = f * modes
        both = [wide[i, at : at + 8, :] for i in range(2)]
        inputs = jnp.concatenate(
            [
                jnp.concatenate([part[:, b * HALF : b * HALF + WINDOW] for part in both], axis=1)
                for b in range(blocks)
            ],
            axis=0,
        ).astype(jnp.bfloat16)
        filtered = lax.dot_general(inputs, bands_ref[f], LAST, preferred_element_type=jnp.float32)
        for b in range(blocks):
            filtered_ref[at : at + modes, b * HALF : (b + 1) * HALF] = filtered[8 * b : 8 * b + modes]
    columns = columns_ref[...]
    for b in range(blocks):
        span = slice(b * HALF, (b + 1) * HALF)
        piece = (filtered_ref[:, span] * gain_ref[...]).astype(jnp.bfloat16)
        part = lax.dot_general(piece, columns, FIRST, preferred_element_type=jnp.float32)

        def store(values, span=span):
            field_ref[span, :] = values.astype(jnp.bfloat16)

        add_over_chunks(chunks, total, span, part, store)


def edge_kernel(
    chunks, halo_ref, filtered_ref, bands_ref, gain_ref, columns_ref, field_ref, out_hbm, wide, more, edge, total, sems
):
    rows, steps = filtered_ref.shape
    freqs = bands_ref.shape[0]
    modes = rows // freqs
    after = lax.axis_index("tm") == 0
    place = pl.multiple_of(jnp.where(after, steps - HALF, 0), HALF)
    rest = pl.multiple_of(jnp.where(after, 0, HALF), HALF)
    reach = pl.multiple_of(jnp.where(after, WINDOW - HALF, 0), HALF)
    first = pltpu.make_async_copy(
        field_ref.at[pl.ds(rest, steps - HALF)], out_hbm.at[pl.ds(rest, steps - HALF)], sems.at[0]
    )
    last = pltpu.make_async_copy(edge, out_hbm.at[pl.ds(place, HALF)], sems.at[1])
    if chunks == 1:
        first.start()
    cells = halo_ref[...].astype(jnp.float32)
    for i, part in enumerate((cells, turned(cells))):
        wide[i, :rows, :] = part
        wide[i, rows:, :] = jnp.zeros((8, HALF), jnp.float32)
    for f in range(freqs):
        at = f * modes
        inputs = jnp.concatenate([wide[i, at : at + 8, :] for i in range(2)], axis=1).astype(jnp.bfloat16)
        taps = jnp.concatenate(
            [bands_ref[f, :, pl.ds(pl.multiple_of(reach + i * WINDOW, HALF), HALF)] for i in range(2)], axis=1
        )
        filtered = lax.dot_general(inputs, taps, LAST, preferred_element_type=jnp.float32)
        more[at : at + modes, :] = filtered[:modes]
    piece = ((filtered_ref[:, pl.ds(place, HALF)] + more[...]) * gain_ref[...]).astype(jnp.bfloat16)
    part = lax.dot_general(piece, columns_ref[...], FIRST, preferred_element_type=jnp.float32)

    def store(values):
        edge[...] = values.astype(jnp.bfloat16)
        last.start()
        if chunks > 1:
            first.start()
        first.wait()
        last.wait()

    add_over_chunks(chunks, total, slice(0, HALF), part, store)


def band_field(coeffs, halo, bands, gain, columns):
    rows, steps = coeffs.shape
    dofs = columns.shape[1]
    freqs = bands.shape[0]
    chunk = min(CHUNK, freqs)
    chunks = freqs // chunk
    one = chunks == 1
    held = rows // chunks
    grid = () if one else (chunks,)
    made = pltpu.VMEM if one else jax.ShapeDtypeStruct

    def rows_of(width):
        return WHOLE if one else pl.BlockSpec((held, width), lambda i: (i, 0))

    taps = WHOLE if one else pl.BlockSpec((chunk, HALF, 2 * WINDOW), lambda i: (i, 0, 0))
    params = pltpu.CompilerParams(vmem_limit_bytes=24 << 20)
    filtered, field = pl.pallas_call(
        functools.partial(own_kernel, chunks),
        grid=grid,
        out_shape=[made((rows, steps), jnp.float32), made((steps, dofs), jnp.bfloat16)],
        in_specs=[rows_of(steps), taps, rows_of(HALF), rows_of(dofs)],
        out_specs=[rows_of(steps), WHOLE],
        scratch_shapes=[
            pltpu.VMEM((2, held + 8, steps + 2 * HALF), jnp.float32),
            pltpu.VMEM((8 if one else steps, dofs), jnp.float32),
        ],
        compiler_params=params,
        cost_estimate=pl.CostEstimate(
            flops=2 * rows * dofs * steps, bytes_accessed=2 * steps * dofs, transcendentals=0
        ),
        name="own_field",
    )(coeffs, bands, gain, columns)
    return pl.pallas_call(
        functools.partial(edge_kernel, chunks),
        grid=grid,
        out_shape=jax.ShapeDtypeStruct((steps, dofs), jnp.bfloat16),
        in_specs=[rows_of(HALF), rows_of(steps), taps, rows_of(HALF), rows_of(dofs), WHOLE],
        out_specs=pl.BlockSpec(memory_space=pl.ANY),
        scratch_shapes=[
            pltpu.VMEM((2, held + 8, HALF), jnp.float32),
            pltpu.VMEM((held, HALF), jnp.float32),
            pltpu.VMEM((HALF, dofs), jnp.bfloat16),
            pltpu.VMEM((8 if one else HALF, dofs), jnp.float32),
            pltpu.SemaphoreType.DMA((2,)),
        ],
        compiler_params=params,
        cost_estimate=pl.CostEstimate(
            flops=2 * rows * dofs * HALF, bytes_accessed=2 * steps * dofs, transcendentals=0
        ),
        name="edge_field",
    )(halo, filtered, bands, gain, columns, field)


def message_scale(dofs, all_dofs):
    snapshot, column = 6.0, 0.0625 * math.sqrt(8192 / all_dofs)
    return 2.0 ** math.floor(math.log2(65504 / (dofs * snapshot * column)))


def exchanged(values, axis, apart, scale):
    count = lax.axis_size(axis)
    message = (values * scale).astype(jnp.float16)
    other = lax.ppermute(message, axis, [(i, i ^ apart) for i in range(count)])
    return values + other.astype(jnp.float32) * (1 / scale)


def per_device(snapshots, mode_columns, filter_taps, mode_gain):
    columns = mode_columns.T
    devices = lax.axis_size("space")
    dofs = columns.shape[1]
    taps = padded_taps(filter_taps)
    gain = jnp.broadcast_to(mode_gain[:, None], (mode_gain.shape[0], HALF))
    coeffs = coefficients(columns, snapshots)
    apart = 1
    while 2 * apart < devices:
        if apart == 2:
            coeffs, taps = lax.optimization_barrier((coeffs, taps))
        coeffs = exchanged(coeffs, "space", apart, message_scale(dofs * apart, dofs * devices))
        apart *= 2
    bands = band_matrices(taps)
    coeffs, bands, gain = lax.optimization_barrier((coeffs, bands, gain))
    coeffs = exchanged(coeffs, "space", apart, message_scale(dofs * apart, dofs * devices))
    edge = jnp.where(lax.axis_index("tm") == 0, coeffs[:, -HALF:], coeffs[:, :HALF])
    halo = lax.ppermute(edge.astype(jnp.bfloat16), "tm", [(0, 1), (1, 0)])
    return band_field(coeffs, halo, bands, gain, columns)


def solution(mesh):
    placed = (P(("group", "tm"), "space"), P("space", "group"), P(), P("group"))
    return jax.shard_map(
        per_device,
        mesh=mesh,
        in_specs=placed,
        out_specs=P(("group", "tm"), "space"),
        check_vma=False,
    )
```

```python
import functools
import math

import jax
import jax.numpy as jnp
from jax import lax
from jax.experimental import pallas as pl
from jax.experimental.pallas import tpu as pltpu
from jax.sharding import PartitionSpec as P

HALF = 128
WINDOW = 3 * HALF
CHUNK = 8
SPLITS = 4
LAST = (((1,), (1,)), ((), ()))
FIRST = (((0,), (0,)), ((), ()))
WHOLE = pl.BlockSpec(memory_space=pltpu.VMEM)


def coefficient_kernel(columns_hbm, snapshots_hbm, out_ref, columns, snapshots, sems):
    width = snapshots.shape[1] // SPLITS
    head = pltpu.make_async_copy(columns_hbm, columns, sems.at[SPLITS])
    head.start()
    copies = []
    for i in range(SPLITS):
        span = pl.ds(i * width, width)
        copies.append(pltpu.make_async_copy(snapshots_hbm.at[:, span], snapshots.at[:, span], sems.at[i]))
        copies[-1].start()
    head.wait()
    total = None
    for i, copy in enumerate(copies):
        copy.wait()
        span = slice(i * width, (i + 1) * width)
        part = lax.dot_general(columns[:, span], snapshots[:, span], LAST, preferred_element_type=jnp.float32)
        total = part if total is None else total + part
    out_ref[...] = total


def coefficients(columns, snapshots):
    rows, dofs = columns.shape
    steps = snapshots.shape[0]
    return pl.pallas_call(
        coefficient_kernel,
        out_shape=pltpu.VMEM((rows, steps), jnp.float32),
        in_specs=[pl.BlockSpec(memory_space=pltpu.HBM)] * 2,
        out_specs=WHOLE,
        scratch_shapes=[
            pltpu.VMEM((rows, dofs), jnp.bfloat16),
            pltpu.VMEM((steps, dofs), jnp.bfloat16),
            pltpu.SemaphoreType.DMA((SPLITS + 1,)),
        ],
        compiler_params=pltpu.CompilerParams(vmem_limit_bytes=16 << 20),
        cost_estimate=pl.CostEstimate(
            flops=2 * rows * dofs * steps, bytes_accessed=2 * steps * dofs, transcendentals=0
        ),
        name="coefficients",
    )(pltpu.with_memory_space_constraint(columns, pltpu.HBM), pltpu.with_memory_space_constraint(snapshots, pltpu.HBM))


def band_kernel(taps_ref, out_ref):
    for f in range(out_ref.shape[0]):
        for part in range(2):
            row = taps_ref[2 * f + part : 2 * f + part + 1, :]
            square = jnp.broadcast_to(row, (HALF, WINDOW))
            out_ref[f, :, part * WINDOW : (part + 1) * WINDOW] = pltpu.roll(
                square, 0, 1, stride=1, stride_axis=0
            ).astype(jnp.bfloat16)


def padded_taps(filter_taps):
    freqs, parts, taps = filter_taps.shape
    rows = filter_taps.astype(jnp.float32).reshape(freqs * parts, taps)
    return jnp.pad(rows, ((0, 0), (0, WINDOW - taps)))


def band_matrices(taps):
    freqs = taps.shape[0] // 2
    chunk = min(CHUNK, freqs)
    one = freqs == chunk
    shape = (freqs, HALF, 2 * WINDOW)
    return pl.pallas_call(
        band_kernel,
        grid=() if one else (freqs // chunk,),
        out_shape=pltpu.VMEM(shape, jnp.bfloat16) if one else jax.ShapeDtypeStruct(shape, jnp.bfloat16),
        in_specs=[WHOLE if one else pl.BlockSpec((2 * chunk, WINDOW), lambda i: (i, 0))],
        out_specs=WHOLE if one else pl.BlockSpec((chunk, HALF, 2 * WINDOW), lambda i: (i, 0, 0)),
        compiler_params=pltpu.CompilerParams(vmem_limit_bytes=16 << 20),
        cost_estimate=pl.CostEstimate(
            flops=freqs * HALF * WINDOW * 40, bytes_accessed=freqs * HALF * WINDOW * 4, transcendentals=0
        ),
        name="band_matrices",
    )(taps)


def turned(cells):
    cosine = lax.broadcasted_iota(jnp.int32, cells.shape, 0) % 2 == 0
    return jnp.where(cosine, -pltpu.roll(cells, cells.shape[0] - 1, 0), pltpu.roll(cells, 1, 0))


def add_over_chunks(chunks, total, span, part, store):
    if chunks == 1:
        store(part)
        return
    step = pl.program_id(0)
    total[span, :] = jnp.where(step == 0, part, total[span, :] + part)

    @pl.when(step == chunks - 1)
    def _():
        store(total[span, :])


def own_kernel(chunks, parts, coeffs_ref, *refs):
    bands, (gain_ref, columns_ref, filtered_ref, field_ref, wide, total) = refs[:parts], refs[parts:]
    rows, steps = coeffs_ref.shape
    blocks = steps // HALF
    each = bands[0].shape[0]
    freqs = parts * each
    modes = rows // freqs
    cells = coeffs_ref[...].astype(jnp.bfloat16).astype(jnp.float32)
    for i, part in enumerate((cells, turned(cells))):
        wide[i, :, :HALF] = jnp.zeros((rows + 8, HALF), jnp.float32)
        wide[i, :, HALF + steps :] = jnp.zeros((rows + 8, HALF), jnp.float32)
        wide[i, :rows, HALF : HALF + steps] = part
        wide[i, rows:, HALF : HALF + steps] = jnp.zeros((8, steps), jnp.float32)
    for f in range(freqs):
        at = f * modes
        both = [wide[i, at : at + 8, :] for i in range(2)]
        inputs = jnp.concatenate(
            [
                jnp.concatenate([part[:, b * HALF : b * HALF + WINDOW] for part in both], axis=1)
                for b in range(blocks)
            ],
            axis=0,
        ).astype(jnp.bfloat16)
        band = bands[f // each][f % each]
        filtered = lax.dot_general(inputs, band, LAST, preferred_element_type=jnp.float32)
        for b in range(blocks):
            filtered_ref[at : at + modes, b * HALF : (b + 1) * HALF] = filtered[8 * b : 8 * b + modes]
    columns = columns_ref[...]
    for b in range(blocks):
        span = slice(b * HALF, (b + 1) * HALF)
        piece = (filtered_ref[:, span] * gain_ref[...]).astype(jnp.bfloat16)
        part = lax.dot_general(piece, columns, FIRST, preferred_element_type=jnp.float32)

        def store(values, span=span):
            field_ref[span, :] = values.astype(jnp.bfloat16)

        add_over_chunks(chunks, total, span, part, store)


def edge_kernel(chunks, parts, halo_ref, filtered_ref, *refs):
    bands, refs = refs[:parts], refs[parts:]
    gain_ref, columns_ref, field_ref, out_hbm, wide, more, edge, total, sems = refs
    rows, steps = filtered_ref.shape
    each = bands[0].shape[0]
    freqs = parts * each
    modes = rows // freqs
    after = lax.axis_index("tm") == 0
    place = pl.multiple_of(jnp.where(after, steps - HALF, 0), HALF)
    rest = pl.multiple_of(jnp.where(after, 0, HALF), HALF)
    reach = pl.multiple_of(jnp.where(after, WINDOW - HALF, 0), HALF)
    first = pltpu.make_async_copy(
        field_ref.at[pl.ds(rest, steps - HALF)], out_hbm.at[pl.ds(rest, steps - HALF)], sems.at[0]
    )
    last = pltpu.make_async_copy(edge, out_hbm.at[pl.ds(place, HALF)], sems.at[1])
    if chunks == 1:
        first.start()
    cells = halo_ref[...].astype(jnp.float32)
    for i, part in enumerate((cells, turned(cells))):
        wide[i, :rows, :] = part
        wide[i, rows:, :] = jnp.zeros((8, HALF), jnp.float32)
    for f in range(freqs):
        at = f * modes
        inputs = jnp.concatenate([wide[i, at : at + 8, :] for i in range(2)], axis=1).astype(jnp.bfloat16)
        taps = jnp.concatenate(
            [
                bands[f // each][f % each, :, pl.ds(pl.multiple_of(reach + i * WINDOW, HALF), HALF)]
                for i in range(2)
            ],
            axis=1,
        )
        filtered = lax.dot_general(inputs, taps, LAST, preferred_element_type=jnp.float32)
        more[at : at + modes, :] = filtered[:modes]
    piece = ((filtered_ref[:, pl.ds(place, HALF)] + more[...]) * gain_ref[...]).astype(jnp.bfloat16)
    part = lax.dot_general(piece, columns_ref[...], FIRST, preferred_element_type=jnp.float32)

    def store(values):
        edge[...] = values.astype(jnp.bfloat16)
        last.start()
        if chunks > 1:
            first.start()
        first.wait()
        last.wait()

    add_over_chunks(chunks, total, slice(0, HALF), part, store)


def band_field(coeffs, halo, bands, gain, columns):
    rows, steps = coeffs.shape
    dofs = columns.shape[1]
    freqs = sum(part.shape[0] for part in bands)
    chunk = min(CHUNK, freqs)
    chunks = freqs // chunk
    one = chunks == 1
    bands = bands if one else [jnp.concatenate(bands)]
    parts = len(bands)
    held = rows // chunks
    grid = () if one else (chunks,)
    made = pltpu.VMEM if one else jax.ShapeDtypeStruct

    def rows_of(width):
        return WHOLE if one else pl.BlockSpec((held, width), lambda i: (i, 0))

    taps = [WHOLE if one else pl.BlockSpec((chunk, HALF, 2 * WINDOW), lambda i: (i, 0, 0))] * parts
    params = pltpu.CompilerParams(vmem_limit_bytes=24 << 20)
    filtered, field = pl.pallas_call(
        functools.partial(own_kernel, chunks, parts),
        grid=grid,
        out_shape=[made((rows, steps), jnp.float32), made((steps, dofs), jnp.bfloat16)],
        in_specs=[rows_of(steps), *taps, rows_of(HALF), rows_of(dofs)],
        out_specs=[rows_of(steps), WHOLE],
        scratch_shapes=[
            pltpu.VMEM((2, held + 8, steps + 2 * HALF), jnp.float32),
            pltpu.VMEM((8 if one else steps, dofs), jnp.float32),
        ],
        compiler_params=params,
        cost_estimate=pl.CostEstimate(
            flops=2 * rows * dofs * steps, bytes_accessed=2 * steps * dofs, transcendentals=0
        ),
        name="own_field",
    )(coeffs, *bands, gain, columns)
    return pl.pallas_call(
        functools.partial(edge_kernel, chunks, parts),
        grid=grid,
        out_shape=jax.ShapeDtypeStruct((steps, dofs), jnp.bfloat16),
        in_specs=[rows_of(HALF), rows_of(steps), *taps, rows_of(HALF), rows_of(dofs), WHOLE],
        out_specs=pl.BlockSpec(memory_space=pl.ANY),
        scratch_shapes=[
            pltpu.VMEM((2, held + 8, HALF), jnp.float32),
            pltpu.VMEM((held, HALF), jnp.float32),
            pltpu.VMEM((HALF, dofs), jnp.bfloat16),
            pltpu.VMEM((8 if one else HALF, dofs), jnp.float32),
            pltpu.SemaphoreType.DMA((2,)),
        ],
        compiler_params=params,
        cost_estimate=pl.CostEstimate(
            flops=2 * rows * dofs * HALF, bytes_accessed=2 * steps * dofs, transcendentals=0
        ),
        name="edge_field",
    )(halo, filtered, *bands, gain, columns, field)


def message_scale(dofs, all_dofs):
    snapshot, column = 6.0, 0.0625 * math.sqrt(8192 / all_dofs)
    return 2.0 ** math.floor(math.log2(65504 / (dofs * snapshot * column)))


def received(message, masks, swap):
    count, cores = lax.axis_size("space"), lax.axis_size("tm")
    others = []
    for mask in masks:
        pairs = [
            (place * cores + core, (place ^ mask) * cores + (core ^ swap))
            for place in range(count)
            for core in range(cores)
        ]
        others.append(lax.ppermute(message, ("space", "tm"), pairs))
    return others


def exchanged(values, masks, scale, swap):
    message = (values * scale).astype(jnp.float16)
    message, values = lax.optimization_barrier((message, values))
    if swap:
        values = lax.ppermute(values, "tm", [(0, 1), (1, 0)])
    others = received(message, masks, swap)
    more = sum(other.astype(jnp.float32) for other in others)
    return values + more * (1 / scale)


def per_device(snapshots, mode_columns, filter_taps, mode_gain):
    columns = mode_columns.T
    devices = lax.axis_size("space")
    dofs = columns.shape[1]
    coeffs = coefficients(columns, snapshots)
    coeffs = exchanged(coeffs, (1, 2, 3), message_scale(dofs, dofs * devices), 1)
    gain = jnp.broadcast_to(mode_gain[:, None], (mode_gain.shape[0], HALF))
    taps, gain = lax.optimization_barrier((padded_taps(filter_taps), gain))
    bands = band_matrices(taps)
    coeffs, bands = lax.optimization_barrier((coeffs, bands))
    apart = 4
    while 2 * apart < devices:
        coeffs = exchanged(coeffs, (apart,), message_scale(dofs * apart, dofs * devices), 0)
        apart *= 2
    coeffs = exchanged(coeffs, (apart,), message_scale(dofs * apart, dofs * devices), 1)
    edge = jnp.where(lax.axis_index("tm") == 0, coeffs[:, -HALF:], coeffs[:, :HALF])
    halo = lax.ppermute(edge.astype(jnp.bfloat16), "tm", [(0, 1), (1, 0)])
    return band_field(coeffs, halo, [bands], gain, columns)


def solution(mesh):
    placed = (P(("group", "tm"), "space"), P("space", "group"), P(), P("group"))
    return jax.shard_map(
        per_device,
        mesh=mesh,
        in_specs=placed,
        out_specs=P(("group", "tm"), "space"),
        check_vma=False,
    )
```

```python
import functools
import math

import jax
import jax.numpy as jnp
from jax import lax
from jax.experimental import pallas as pl
from jax.experimental.pallas import tpu as pltpu
from jax.sharding import PartitionSpec as P

HALF = 128
WINDOW = 3 * HALF
CHUNK = 8
SPLITS = 4
LAST = (((1,), (1,)), ((), ()))
FIRST = (((0,), (0,)), ((), ()))
WHOLE = pl.BlockSpec(memory_space=pltpu.VMEM)


def coefficient_kernel(columns_hbm, snapshots_hbm, out_ref, columns, snapshots, sems):
    width = snapshots.shape[1] // SPLITS
    head = pltpu.make_async_copy(columns_hbm, columns, sems.at[SPLITS])
    head.start()
    copies = []
    for i in range(SPLITS):
        span = pl.ds(i * width, width)
        copies.append(pltpu.make_async_copy(snapshots_hbm.at[:, span], snapshots.at[:, span], sems.at[i]))
        copies[-1].start()
    head.wait()
    total = None
    for i, copy in enumerate(copies):
        copy.wait()
        span = slice(i * width, (i + 1) * width)
        part = lax.dot_general(columns[:, span], snapshots[:, span], LAST, preferred_element_type=jnp.float32)
        total = part if total is None else total + part
    out_ref[...] = total


def coefficients(columns, snapshots):
    rows, dofs = columns.shape
    steps = snapshots.shape[0]
    return pl.pallas_call(
        coefficient_kernel,
        out_shape=pltpu.VMEM((rows, steps), jnp.float32),
        in_specs=[pl.BlockSpec(memory_space=pltpu.HBM)] * 2,
        out_specs=WHOLE,
        scratch_shapes=[
            pltpu.VMEM((rows, dofs), jnp.bfloat16),
            pltpu.VMEM((steps, dofs), jnp.bfloat16),
            pltpu.SemaphoreType.DMA((SPLITS + 1,)),
        ],
        compiler_params=pltpu.CompilerParams(vmem_limit_bytes=16 << 20),
        cost_estimate=pl.CostEstimate(
            flops=2 * rows * dofs * steps, bytes_accessed=2 * steps * dofs, transcendentals=0
        ),
        name="coefficients",
    )(pltpu.with_memory_space_constraint(columns, pltpu.HBM), pltpu.with_memory_space_constraint(snapshots, pltpu.HBM))


def band_kernel(taps_ref, out_ref):
    for f in range(out_ref.shape[0]):
        for part in range(2):
            row = taps_ref[2 * f + part : 2 * f + part + 1, :]
            square = jnp.broadcast_to(row, (HALF, WINDOW))
            out_ref[f, :, part * WINDOW : (part + 1) * WINDOW] = pltpu.roll(
                square, 0, 1, stride=1, stride_axis=0
            ).astype(jnp.bfloat16)


def padded_taps(filter_taps):
    freqs, parts, taps = filter_taps.shape
    rows = filter_taps.astype(jnp.float32).reshape(freqs * parts, taps)
    return jnp.pad(rows, ((0, 0), (0, WINDOW - taps)))


def band_matrices(taps):
    freqs = taps.shape[0] // 2
    chunk = min(CHUNK, freqs)
    one = freqs == chunk
    shape = (freqs, HALF, 2 * WINDOW)
    return pl.pallas_call(
        band_kernel,
        grid=() if one else (freqs // chunk,),
        out_shape=pltpu.VMEM(shape, jnp.bfloat16) if one else jax.ShapeDtypeStruct(shape, jnp.bfloat16),
        in_specs=[WHOLE if one else pl.BlockSpec((2 * chunk, WINDOW), lambda i: (i, 0))],
        out_specs=WHOLE if one else pl.BlockSpec((chunk, HALF, 2 * WINDOW), lambda i: (i, 0, 0)),
        compiler_params=pltpu.CompilerParams(vmem_limit_bytes=16 << 20),
        cost_estimate=pl.CostEstimate(
            flops=freqs * HALF * WINDOW * 40, bytes_accessed=freqs * HALF * WINDOW * 4, transcendentals=0
        ),
        name="band_matrices",
    )(taps)


def turned(cells):
    cosine = lax.broadcasted_iota(jnp.int32, cells.shape, 0) % 2 == 0
    return jnp.where(cosine, -pltpu.roll(cells, cells.shape[0] - 1, 0), pltpu.roll(cells, 1, 0))


def add_over_chunks(chunks, total, span, part, store):
    if chunks == 1:
        store(part)
        return
    step = pl.program_id(0)
    total[span] = jnp.where(step == 0, part, total[span] + part)

    @pl.when(step == chunks - 1)
    def _():
        store(total[span])


def places(steps):
    after = lax.axis_index("tm") == 0
    rest = pl.multiple_of(jnp.where(after, 0, HALF), HALF)
    return rest, pl.multiple_of(jnp.where(after, steps - HALF, 0), HALF)


def own_kernel(chunks, parts, coeffs_ref, *refs):
    bands, (gain_ref, columns_ref, filtered_ref, field_ref, wide, total) = refs[:parts], refs[parts:]
    rows, steps = coeffs_ref.shape
    blocks = steps // HALF
    each = bands[0].shape[0]
    freqs = parts * each
    modes = rows // freqs
    cells = coeffs_ref[...].astype(jnp.bfloat16).astype(jnp.float32)
    for i, part in enumerate((cells, turned(cells))):
        wide[i, :, :HALF] = jnp.zeros((rows + 8, HALF), jnp.float32)
        wide[i, :, HALF + steps :] = jnp.zeros((rows + 8, HALF), jnp.float32)
        wide[i, :rows, HALF : HALF + steps] = part
        wide[i, rows:, HALF : HALF + steps] = jnp.zeros((8, steps), jnp.float32)
    for f in range(freqs):
        at = f * modes
        both = [wide[i, at : at + 8, :] for i in range(2)]
        inputs = jnp.concatenate(
            [
                jnp.concatenate([part[:, b * HALF : b * HALF + WINDOW] for part in both], axis=1)
                for b in range(blocks)
            ],
            axis=0,
        ).astype(jnp.bfloat16)
        band = bands[f // each][f % each]
        filtered = lax.dot_general(inputs, band, LAST, preferred_element_type=jnp.float32)
        for b in range(blocks):
            filtered_ref[at : at + modes, b * HALF : (b + 1) * HALF] = filtered[8 * b : 8 * b + modes]
    columns = columns_ref[...]
    rest, _ = places(steps)
    for b in range(blocks - 1):
        span = pl.ds(pl.multiple_of(rest + b * HALF, HALF), HALF)
        piece = (filtered_ref[:, span] * gain_ref[...]).astype(jnp.bfloat16)
        part = lax.dot_general(piece, columns, FIRST, preferred_element_type=jnp.float32)

        def store(values, span=span):
            field_ref[span, :] = values.astype(jnp.bfloat16)

        add_over_chunks(chunks, total, (span, slice(None)), part, store)


def edge_kernel(chunks, parts, halo_ref, filtered_ref, *refs):
    bands, refs = refs[:parts], refs[parts:]
    gain_ref, columns_ref, field_ref, out_hbm, wide, more, edge, total, sems = refs
    rows, steps = filtered_ref.shape
    each = bands[0].shape[0]
    freqs = parts * each
    modes = rows // freqs
    rest, place = places(steps)
    reach = pl.multiple_of(jnp.where(rest == 0, WINDOW - HALF, 0), HALF)
    first = pltpu.make_async_copy(
        field_ref.at[pl.ds(rest, steps - HALF)], out_hbm.at[pl.ds(rest, steps - HALF)], sems.at[0]
    )
    if chunks == 1:
        first.start()
    cells = halo_ref[...].astype(jnp.float32)
    for i, part in enumerate((cells, turned(cells))):
        wide[i, :rows, :] = part
        wide[i, rows:, :] = jnp.zeros((8, HALF), jnp.float32)
    for f in range(freqs):
        at = f * modes
        inputs = jnp.concatenate([wide[i, at : at + 8, :] for i in range(2)], axis=1).astype(jnp.bfloat16)
        taps = jnp.concatenate(
            [
                bands[f // each][f % each, :, pl.ds(pl.multiple_of(reach + i * WINDOW, HALF), HALF)]
                for i in range(2)
            ],
            axis=1,
        )
        filtered = lax.dot_general(inputs, taps, LAST, preferred_element_type=jnp.float32)
        more[at : at + modes, :] = filtered[:modes]
    piece = ((filtered_ref[:, pl.ds(place, HALF)] + more[...]) * gain_ref[...]).astype(jnp.bfloat16)
    width = columns_ref.shape[1] // SPLITS
    copies = [first]
    for i in range(SPLITS):
        span = (slice(None), slice(i * width, (i + 1) * width))
        part = lax.dot_general(piece, columns_ref[span], FIRST, preferred_element_type=jnp.float32)
        target = out_hbm.at[pl.ds(place, HALF), pl.ds(i * width, width)]
        copies.append(pltpu.make_async_copy(edge.at[span], target, sems.at[1 + i]))

        def store(values, span=span, copy=copies[-1]):
            edge[span] = values.astype(jnp.bfloat16)
            copy.start()

        add_over_chunks(chunks, total, span, part, store)

    def finish():
        if chunks > 1:
            first.start()
        for copy in copies:
            copy.wait()

    if chunks == 1:
        finish()
    else:
        pl.when(pl.program_id(0) == chunks - 1)(finish)


def band_field(coeffs, halo, bands, gain, columns):
    rows, steps = coeffs.shape
    dofs = columns.shape[1]
    freqs = sum(part.shape[0] for part in bands)
    chunk = min(CHUNK, freqs)
    chunks = freqs // chunk
    one = chunks == 1
    bands = bands if one else [jnp.concatenate(bands)]
    parts = len(bands)
    held = rows // chunks
    grid = () if one else (chunks,)
    made = pltpu.VMEM if one else jax.ShapeDtypeStruct

    def rows_of(width):
        return WHOLE if one else pl.BlockSpec((held, width), lambda i: (i, 0))

    taps = [WHOLE if one else pl.BlockSpec((chunk, HALF, 2 * WINDOW), lambda i: (i, 0, 0))] * parts
    params = pltpu.CompilerParams(vmem_limit_bytes=24 << 20)
    filtered, field = pl.pallas_call(
        functools.partial(own_kernel, chunks, parts),
        grid=grid,
        out_shape=[made((rows, steps), jnp.float32), made((steps, dofs), jnp.bfloat16)],
        in_specs=[rows_of(steps), *taps, rows_of(HALF), rows_of(dofs)],
        out_specs=[rows_of(steps), WHOLE],
        scratch_shapes=[
            pltpu.VMEM((2, held + 8, steps + 2 * HALF), jnp.float32),
            pltpu.VMEM((8 if one else steps, dofs), jnp.float32),
        ],
        compiler_params=params,
        cost_estimate=pl.CostEstimate(
            flops=2 * rows * dofs * steps, bytes_accessed=2 * steps * dofs, transcendentals=0
        ),
        name="own_field",
    )(coeffs, *bands, gain, columns)
    return pl.pallas_call(
        functools.partial(edge_kernel, chunks, parts),
        grid=grid,
        out_shape=jax.ShapeDtypeStruct((steps, dofs), jnp.bfloat16),
        in_specs=[rows_of(HALF), rows_of(steps), *taps, rows_of(HALF), rows_of(dofs), WHOLE],
        out_specs=pl.BlockSpec(memory_space=pl.ANY),
        scratch_shapes=[
            pltpu.VMEM((2, held + 8, HALF), jnp.float32),
            pltpu.VMEM((held, HALF), jnp.float32),
            pltpu.VMEM((HALF, dofs), jnp.bfloat16),
            pltpu.VMEM((8 if one else HALF, dofs), jnp.float32),
            pltpu.SemaphoreType.DMA((1 + SPLITS,)),
        ],
        compiler_params=params,
        cost_estimate=pl.CostEstimate(
            flops=2 * rows * dofs * HALF, bytes_accessed=2 * steps * dofs, transcendentals=0
        ),
        name="edge_field",
    )(halo, filtered, *bands, gain, columns, field)


def message_scale(dofs, all_dofs):
    snapshot, column = 6.0, 0.0625 * math.sqrt(8192 / all_dofs)
    return 2.0 ** math.floor(math.log2(65504 / (dofs * snapshot * column)))


def received(message, masks, swap):
    count, cores = lax.axis_size("space"), lax.axis_size("tm")
    others = []
    for mask in masks:
        pairs = [
            (place * cores + core, (place ^ mask) * cores + (core ^ swap))
            for place in range(count)
            for core in range(cores)
        ]
        others.append(lax.ppermute(message, ("space", "tm"), pairs))
    return others


def exchanged(values, masks, scale, swap):
    message = (values * scale).astype(jnp.float16)
    others = [lax.ppermute(message, "tm", [(0, 1), (1, 0)])] if swap else []
    others += received(message, masks, swap)
    more = sum(other.astype(jnp.float32) for other in others) * (1 / scale)
    return more if swap else values + more


def per_device(snapshots, mode_columns, filter_taps, mode_gain):
    columns = mode_columns.T
    devices = lax.axis_size("space")
    dofs = columns.shape[1]
    coeffs = coefficients(columns, snapshots)
    coeffs = exchanged(coeffs, (1, 2, 3), message_scale(dofs, dofs * devices), 1)
    gain = jnp.broadcast_to(mode_gain[:, None], (mode_gain.shape[0], HALF))
    taps, gain = lax.optimization_barrier((padded_taps(filter_taps), gain))
    bands = band_matrices(taps)
    coeffs, bands = lax.optimization_barrier((coeffs, bands))
    apart = 4
    while 2 * apart < devices:
        coeffs = exchanged(coeffs, (apart,), message_scale(dofs * apart, dofs * devices), 0)
        apart *= 2
    coeffs = exchanged(coeffs, (apart,), message_scale(dofs * apart, dofs * devices), 1)
    edge = jnp.where(lax.axis_index("tm") == 0, coeffs[:, -HALF:], coeffs[:, :HALF])
    halo = lax.ppermute(edge.astype(jnp.bfloat16), "tm", [(0, 1), (1, 0)])
    return band_field(coeffs, halo, [bands], gain, columns)


def solution(mesh):
    placed = (P(("group", "tm"), "space"), P("space", "group"), P(), P("group"))
    return jax.shard_map(
        per_device,
        mesh=mesh,
        in_specs=placed,
        out_specs=P(("group", "tm"), "space"),
        check_vma=False,
    )
```

```python
import functools
import math

import jax
import jax.numpy as jnp
from jax import lax
from jax.experimental import pallas as pl
from jax.experimental.pallas import tpu as pltpu
from jax.sharding import PartitionSpec as P

HALF = 128
WINDOW = 3 * HALF
CHUNK = 8
SPLITS = 4
LAST = (((1,), (1,)), ((), ()))
FIRST = (((0,), (0,)), ((), ()))
WHOLE = pl.BlockSpec(memory_space=pltpu.VMEM)


def coefficient_kernel(columns_hbm, snapshots_hbm, out_ref, columns, snapshots, sems):
    width = snapshots.shape[1] // SPLITS
    head = pltpu.make_async_copy(columns_hbm, columns, sems.at[SPLITS])
    head.start()
    copies = []
    for i in range(SPLITS):
        span = pl.ds(i * width, width)
        copies.append(pltpu.make_async_copy(snapshots_hbm.at[:, span], snapshots.at[:, span], sems.at[i]))
        copies[-1].start()
    head.wait()
    total = None
    for i, copy in enumerate(copies):
        copy.wait()
        span = slice(i * width, (i + 1) * width)
        part = lax.dot_general(columns[:, span], snapshots[:, span], LAST, preferred_element_type=jnp.float32)
        total = part if total is None else total + part
    out_ref[...] = total


def coefficients(columns, snapshots):
    rows, dofs = columns.shape
    steps = snapshots.shape[0]
    return pl.pallas_call(
        coefficient_kernel,
        out_shape=pltpu.VMEM((rows, steps), jnp.float32),
        in_specs=[pl.BlockSpec(memory_space=pltpu.HBM)] * 2,
        out_specs=WHOLE,
        scratch_shapes=[
            pltpu.VMEM((rows, dofs), jnp.bfloat16),
            pltpu.VMEM((steps, dofs), jnp.bfloat16),
            pltpu.SemaphoreType.DMA((SPLITS + 1,)),
        ],
        compiler_params=pltpu.CompilerParams(vmem_limit_bytes=16 << 20),
        cost_estimate=pl.CostEstimate(
            flops=2 * rows * dofs * steps, bytes_accessed=2 * steps * dofs, transcendentals=0
        ),
        name="coefficients",
    )(pltpu.with_memory_space_constraint(columns, pltpu.HBM), pltpu.with_memory_space_constraint(snapshots, pltpu.HBM))


def band_kernel(taps_ref, out_ref):
    for f in range(out_ref.shape[0]):
        for part in range(2):
            row = taps_ref[2 * f + part : 2 * f + part + 1, :]
            square = jnp.broadcast_to(row, (HALF, WINDOW))
            out_ref[f, :, part * WINDOW : (part + 1) * WINDOW] = pltpu.roll(
                square, 0, 1, stride=1, stride_axis=0
            ).astype(jnp.bfloat16)


def padded_taps(filter_taps):
    freqs, parts, taps = filter_taps.shape
    rows = filter_taps.astype(jnp.float32).reshape(freqs * parts, taps)
    return jnp.pad(rows, ((0, 0), (0, WINDOW - taps)))


def band_matrices(taps):
    freqs = taps.shape[0] // 2
    chunk = min(CHUNK, freqs)
    one = freqs == chunk
    shape = (freqs, HALF, 2 * WINDOW)
    return pl.pallas_call(
        band_kernel,
        grid=() if one else (freqs // chunk,),
        out_shape=pltpu.VMEM(shape, jnp.bfloat16) if one else jax.ShapeDtypeStruct(shape, jnp.bfloat16),
        in_specs=[WHOLE if one else pl.BlockSpec((2 * chunk, WINDOW), lambda i: (i, 0))],
        out_specs=WHOLE if one else pl.BlockSpec((chunk, HALF, 2 * WINDOW), lambda i: (i, 0, 0)),
        compiler_params=pltpu.CompilerParams(vmem_limit_bytes=16 << 20),
        cost_estimate=pl.CostEstimate(
            flops=freqs * HALF * WINDOW * 40, bytes_accessed=freqs * HALF * WINDOW * 4, transcendentals=0
        ),
        name="band_matrices",
    )(taps)


def turned(cells):
    cosine = lax.broadcasted_iota(jnp.int32, cells.shape, 0) % 2 == 0
    return jnp.where(cosine, -pltpu.roll(cells, cells.shape[0] - 1, 0), pltpu.roll(cells, 1, 0))


def add_over_chunks(chunks, total, span, part, store):
    if chunks == 1:
        store(part)
        return
    step = pl.program_id(0)
    total[span] = jnp.where(step == 0, part, total[span] + part)

    @pl.when(step == chunks - 1)
    def _():
        store(total[span])


def places(steps):
    after = lax.axis_index("tm") == 0
    rest = pl.multiple_of(jnp.where(after, 0, HALF), HALF)
    return rest, pl.multiple_of(jnp.where(after, steps - HALF, 0), HALF)


def own_kernel(chunks, parts, coeffs_ref, *refs):
    bands, (gain_ref, columns_ref, filtered_ref, field_ref, wide, total) = refs[:parts], refs[parts:]
    rows, steps = coeffs_ref.shape
    blocks = steps // HALF
    each = bands[0].shape[0]
    freqs = parts * each
    modes = rows // freqs
    cells = coeffs_ref[...].astype(jnp.bfloat16).astype(jnp.float32)
    for i, part in enumerate((cells, turned(cells))):
        wide[i, :, :HALF] = jnp.zeros((rows + 8, HALF), jnp.float32)
        wide[i, :, HALF + steps :] = jnp.zeros((rows + 8, HALF), jnp.float32)
        wide[i, :rows, HALF : HALF + steps] = part
        wide[i, rows:, HALF : HALF + steps] = jnp.zeros((8, steps), jnp.float32)
    for f in range(freqs):
        at = f * modes
        both = [wide[i, at : at + 8, :] for i in range(2)]
        inputs = jnp.concatenate(
            [
                jnp.concatenate([part[:, b * HALF : b * HALF + WINDOW] for part in both], axis=1)
                for b in range(blocks)
            ],
            axis=0,
        ).astype(jnp.bfloat16)
        band = bands[f // each][f % each]
        filtered = lax.dot_general(inputs, band, LAST, preferred_element_type=jnp.float32)
        for b in range(blocks):
            filtered_ref[at : at + modes, b * HALF : (b + 1) * HALF] = filtered[8 * b : 8 * b + modes]
    columns = columns_ref[...]
    rest, _ = places(steps)
    for b in range(blocks - 1):
        span = pl.ds(pl.multiple_of(rest + b * HALF, HALF), HALF)
        piece = (filtered_ref[:, span] * gain_ref[...]).astype(jnp.bfloat16)
        part = lax.dot_general(piece, columns, FIRST, preferred_element_type=jnp.float32)

        def store(values, span=span):
            field_ref[span, :] = values.astype(jnp.bfloat16)

        add_over_chunks(chunks, total, (span, slice(None)), part, store)


def edge_kernel(chunks, parts, halo_ref, filtered_ref, *refs):
    bands, refs = refs[:parts], refs[parts:]
    gain_ref, columns_ref, field_ref, out_hbm, wide, more, edge, total, sems = refs
    rows, steps = filtered_ref.shape
    each = bands[0].shape[0]
    freqs = parts * each
    modes = rows // freqs
    rest, place = places(steps)
    reach = pl.multiple_of(jnp.where(rest == 0, WINDOW - HALF, 0), HALF)
    first = pltpu.make_async_copy(
        field_ref.at[pl.ds(rest, steps - HALF)], out_hbm.at[pl.ds(rest, steps - HALF)], sems.at[0]
    )
    if chunks == 1:
        first.start()
    cells = halo_ref[...].astype(jnp.float32)
    for i, part in enumerate((cells, turned(cells))):
        wide[i, :rows, :] = part
        wide[i, rows:, :] = jnp.zeros((8, HALF), jnp.float32)
    for f in range(freqs):
        at = f * modes
        inputs = jnp.concatenate([wide[i, at : at + 8, :] for i in range(2)], axis=1).astype(jnp.bfloat16)
        taps = jnp.concatenate(
            [
                bands[f // each][f % each, :, pl.ds(pl.multiple_of(reach + i * WINDOW, HALF), HALF)]
                for i in range(2)
            ],
            axis=1,
        )
        filtered = lax.dot_general(inputs, taps, LAST, preferred_element_type=jnp.float32)
        more[at : at + modes, :] = filtered[:modes]
    piece = ((filtered_ref[:, pl.ds(place, HALF)] + more[...]) * gain_ref[...]).astype(jnp.bfloat16)
    width = columns_ref.shape[1] // SPLITS
    copies = [first]
    for i in range(SPLITS):
        span = (slice(None), slice(i * width, (i + 1) * width))
        part = lax.dot_general(piece, columns_ref[span], FIRST, preferred_element_type=jnp.float32)
        target = out_hbm.at[pl.ds(place, HALF), pl.ds(i * width, width)]
        copies.append(pltpu.make_async_copy(edge.at[span], target, sems.at[1 + i]))

        def store(values, span=span, copy=copies[-1]):
            edge[span] = values.astype(jnp.bfloat16)
            copy.start()

        add_over_chunks(chunks, total, span, part, store)

    def finish():
        if chunks > 1:
            first.start()
        for copy in copies:
            copy.wait()

    if chunks == 1:
        finish()
    else:
        pl.when(pl.program_id(0) == chunks - 1)(finish)


def band_field(coeffs, halo, bands, gain, columns):
    rows, steps = coeffs.shape
    dofs = columns.shape[1]
    freqs = sum(part.shape[0] for part in bands)
    chunk = min(CHUNK, freqs)
    chunks = freqs // chunk
    one = chunks == 1
    bands = bands if one else [jnp.concatenate(bands)]
    parts = len(bands)
    held = rows // chunks
    grid = () if one else (chunks,)
    made = pltpu.VMEM if one else jax.ShapeDtypeStruct

    def rows_of(width):
        return WHOLE if one else pl.BlockSpec((held, width), lambda i: (i, 0))

    taps = [WHOLE if one else pl.BlockSpec((chunk, HALF, 2 * WINDOW), lambda i: (i, 0, 0))] * parts
    params = pltpu.CompilerParams(vmem_limit_bytes=24 << 20)
    filtered, field = pl.pallas_call(
        functools.partial(own_kernel, chunks, parts),
        grid=grid,
        out_shape=[made((rows, steps), jnp.float32), made((steps, dofs), jnp.bfloat16)],
        in_specs=[rows_of(steps), *taps, rows_of(HALF), rows_of(dofs)],
        out_specs=[rows_of(steps), WHOLE],
        scratch_shapes=[
            pltpu.VMEM((2, held + 8, steps + 2 * HALF), jnp.float32),
            pltpu.VMEM((8 if one else steps, dofs), jnp.float32),
        ],
        compiler_params=params,
        cost_estimate=pl.CostEstimate(
            flops=2 * rows * dofs * steps, bytes_accessed=2 * steps * dofs, transcendentals=0
        ),
        name="own_field",
    )(coeffs, *bands, gain, columns)
    return pl.pallas_call(
        functools.partial(edge_kernel, chunks, parts),
        grid=grid,
        out_shape=jax.ShapeDtypeStruct((steps, dofs), jnp.bfloat16),
        in_specs=[rows_of(HALF), rows_of(steps), *taps, rows_of(HALF), rows_of(dofs), WHOLE],
        out_specs=pl.BlockSpec(memory_space=pl.ANY),
        scratch_shapes=[
            pltpu.VMEM((2, held + 8, HALF), jnp.float32),
            pltpu.VMEM((held, HALF), jnp.float32),
            pltpu.VMEM((HALF, dofs), jnp.bfloat16),
            pltpu.VMEM((8 if one else HALF, dofs), jnp.float32),
            pltpu.SemaphoreType.DMA((1 + SPLITS,)),
        ],
        compiler_params=params,
        cost_estimate=pl.CostEstimate(
            flops=2 * rows * dofs * HALF, bytes_accessed=2 * steps * dofs, transcendentals=0
        ),
        name="edge_field",
    )(halo, filtered, *bands, gain, columns, field)


def message_scale(dofs, all_dofs):
    snapshot, column = 6.0, 0.0625 * math.sqrt(8192 / all_dofs)
    return 2.0 ** math.floor(math.log2(65504 / (dofs * snapshot * column)))


def received(message, masks, swap):
    count, cores = lax.axis_size("space"), lax.axis_size("tm")
    others = []
    for mask in masks:
        pairs = [
            (place * cores + core, (place ^ mask) * cores + (core ^ swap))
            for place in range(count)
            for core in range(cores)
        ]
        others.append(lax.ppermute(message, ("space", "tm"), pairs))
    return others


def exchanged(values, masks, scale, swap, ready=None):
    message = (values * scale).astype(jnp.float16)
    if ready is not None:
        message, ready = lax.optimization_barrier((message, ready))
    others = [lax.ppermute(message, "tm", [(0, 1), (1, 0)])] if swap else []
    others += received(message, masks, swap)
    more = sum(other.astype(jnp.float32) for other in others) * (1 / scale)
    values = more if swap else values + more
    return values if ready is None else (values, ready)


def per_device(snapshots, mode_columns, filter_taps, mode_gain):
    columns = mode_columns.T
    devices = lax.axis_size("space")
    dofs = columns.shape[1]
    coeffs = coefficients(columns, snapshots)
    coeffs = exchanged(coeffs, (4,), message_scale(dofs, dofs * devices), 1)
    gain = jnp.broadcast_to(mode_gain[:, None], (mode_gain.shape[0], HALF))
    taps, gain = lax.optimization_barrier((padded_taps(filter_taps), gain))
    bands = band_matrices(taps)
    apart = 8
    while apart < devices:
        coeffs = exchanged(coeffs, (apart,), message_scale(dofs * apart // 4, dofs * devices), 0)
        apart *= 2
    coeffs, bands = exchanged(coeffs, (1, 2, 3), message_scale(dofs * devices // 4, dofs * devices), 1, bands)
    edge = jnp.where(lax.axis_index("tm") == 0, coeffs[:, -HALF:], coeffs[:, :HALF])
    halo = lax.ppermute(edge.astype(jnp.bfloat16), "tm", [(0, 1), (1, 0)])
    return band_field(coeffs, halo, [bands], gain, columns)


def solution(mesh):
    placed = (P(("group", "tm"), "space"), P("space", "group"), P(), P("group"))
    return jax.shard_map(
        per_device,
        mesh=mesh,
        in_specs=placed,
        out_specs=P(("group", "tm"), "space"),
        check_vma=False,
    )
```

```python
import functools
import math

import jax
import jax.numpy as jnp
from jax import lax
from jax.experimental import pallas as pl
from jax.experimental.pallas import tpu as pltpu
from jax.sharding import PartitionSpec as P

HALF = 128
WINDOW = 3 * HALF
CHUNK = 8
SPLITS = 4
LAST = (((1,), (1,)), ((), ()))
FIRST = (((0,), (0,)), ((), ()))
WHOLE = pl.BlockSpec(memory_space=pltpu.VMEM)


def coefficient_kernel(columns_hbm, snapshots_hbm, out_ref, columns, snapshots, sems):
    width = snapshots.shape[1] // SPLITS
    head = pltpu.make_async_copy(columns_hbm, columns, sems.at[SPLITS])
    head.start()
    copies = []
    for i in range(SPLITS):
        span = pl.ds(i * width, width)
        copies.append(pltpu.make_async_copy(snapshots_hbm.at[:, span], snapshots.at[:, span], sems.at[i]))
        copies[-1].start()
    head.wait()
    total = None
    for i, copy in enumerate(copies):
        copy.wait()
        span = slice(i * width, (i + 1) * width)
        part = lax.dot_general(columns[:, span], snapshots[:, span], LAST, preferred_element_type=jnp.float32)
        total = part if total is None else total + part
    out_ref[...] = total


def coefficients(columns, snapshots):
    rows, dofs = columns.shape
    steps = snapshots.shape[0]
    return pl.pallas_call(
        coefficient_kernel,
        out_shape=pltpu.VMEM((rows, steps), jnp.float32),
        in_specs=[pl.BlockSpec(memory_space=pltpu.HBM)] * 2,
        out_specs=WHOLE,
        scratch_shapes=[
            pltpu.VMEM((rows, dofs), jnp.bfloat16),
            pltpu.VMEM((steps, dofs), jnp.bfloat16),
            pltpu.SemaphoreType.DMA((SPLITS + 1,)),
        ],
        compiler_params=pltpu.CompilerParams(vmem_limit_bytes=16 << 20),
        cost_estimate=pl.CostEstimate(
            flops=2 * rows * dofs * steps, bytes_accessed=2 * steps * dofs, transcendentals=0
        ),
        name="coefficients",
    )(pltpu.with_memory_space_constraint(columns, pltpu.HBM), pltpu.with_memory_space_constraint(snapshots, pltpu.HBM))


def band_kernel(taps_ref, out_ref):
    for f in range(out_ref.shape[0]):
        for part in range(2):
            row = taps_ref[2 * f + part : 2 * f + part + 1, :]
            square = jnp.broadcast_to(row, (HALF, WINDOW))
            out_ref[f, :, part * WINDOW : (part + 1) * WINDOW] = pltpu.roll(
                square, 0, 1, stride=1, stride_axis=0
            ).astype(jnp.bfloat16)


def padded_taps(filter_taps):
    freqs, parts, taps = filter_taps.shape
    rows = filter_taps.astype(jnp.float32).reshape(freqs * parts, taps)
    return jnp.pad(rows, ((0, 0), (0, WINDOW - taps)))


def band_matrices(taps):
    freqs = taps.shape[0] // 2
    chunk = min(CHUNK, freqs)
    one = freqs == chunk
    shape = (freqs, HALF, 2 * WINDOW)
    return pl.pallas_call(
        band_kernel,
        grid=() if one else (freqs // chunk,),
        out_shape=pltpu.VMEM(shape, jnp.bfloat16) if one else jax.ShapeDtypeStruct(shape, jnp.bfloat16),
        in_specs=[WHOLE if one else pl.BlockSpec((2 * chunk, WINDOW), lambda i: (i, 0))],
        out_specs=WHOLE if one else pl.BlockSpec((chunk, HALF, 2 * WINDOW), lambda i: (i, 0, 0)),
        compiler_params=pltpu.CompilerParams(vmem_limit_bytes=16 << 20),
        cost_estimate=pl.CostEstimate(
            flops=freqs * HALF * WINDOW * 40, bytes_accessed=freqs * HALF * WINDOW * 4, transcendentals=0
        ),
        name="band_matrices",
    )(taps)


def turned(cells):
    cosine = lax.broadcasted_iota(jnp.int32, cells.shape, 0) % 2 == 0
    return jnp.where(cosine, -pltpu.roll(cells, cells.shape[0] - 1, 0), pltpu.roll(cells, 1, 0))


def add_over_chunks(chunks, total, span, part, store):
    if chunks == 1:
        store(part)
        return
    step = pl.program_id(0)
    total[span] = jnp.where(step == 0, part, total[span] + part)

    @pl.when(step == chunks - 1)
    def _():
        store(total[span])


def places(steps):
    after = lax.axis_index("tm") == 0
    rest = pl.multiple_of(jnp.where(after, 0, HALF), HALF)
    return rest, pl.multiple_of(jnp.where(after, steps - HALF, 0), HALF)


def own_kernel(chunks, parts, coeffs_ref, *refs):
    bands, (gain_ref, columns_ref, filtered_ref, field_ref, wide, total) = refs[:parts], refs[parts:]
    rows, steps = coeffs_ref.shape
    blocks = steps // HALF
    each = bands[0].shape[0]
    freqs = parts * each
    modes = rows // freqs
    cells = coeffs_ref[...].astype(jnp.bfloat16).astype(jnp.float32)
    for i, part in enumerate((cells, turned(cells))):
        wide[i, :, :HALF] = jnp.zeros((rows + 8, HALF), jnp.float32)
        wide[i, :, HALF + steps :] = jnp.zeros((rows + 8, HALF), jnp.float32)
        wide[i, :rows, HALF : HALF + steps] = part
        wide[i, rows:, HALF : HALF + steps] = jnp.zeros((8, steps), jnp.float32)
    for f in range(freqs):
        at = f * modes
        both = [wide[i, at : at + 8, :] for i in range(2)]
        inputs = jnp.concatenate(
            [
                jnp.concatenate([part[:, b * HALF : b * HALF + WINDOW] for part in both], axis=1)
                for b in range(blocks)
            ],
            axis=0,
        ).astype(jnp.bfloat16)
        band = bands[f // each][f % each]
        filtered = lax.dot_general(inputs, band, LAST, preferred_element_type=jnp.float32)
        for b in range(blocks):
            filtered_ref[at : at + modes, b * HALF : (b + 1) * HALF] = filtered[8 * b : 8 * b + modes]
    columns = columns_ref[...]
    rest, _ = places(steps)
    for b in range(blocks - 1):
        span = pl.ds(pl.multiple_of(rest + b * HALF, HALF), HALF)
        piece = (filtered_ref[:, span] * gain_ref[...]).astype(jnp.bfloat16)
        part = lax.dot_general(piece, columns, FIRST, preferred_element_type=jnp.float32)

        def store(values, span=span):
            field_ref[span, :] = values.astype(jnp.bfloat16)

        add_over_chunks(chunks, total, (span, slice(None)), part, store)


def edge_kernel(chunks, parts, halo_ref, filtered_ref, *refs):
    bands, refs = refs[:parts], refs[parts:]
    gain_ref, columns_ref, field_ref, out_hbm, wide, more, edge, total, sems = refs
    rows, steps = filtered_ref.shape
    each = bands[0].shape[0]
    freqs = parts * each
    modes = rows // freqs
    rest, place = places(steps)
    reach = pl.multiple_of(jnp.where(rest == 0, WINDOW - HALF, 0), HALF)
    first = pltpu.make_async_copy(
        field_ref.at[pl.ds(rest, steps - HALF)], out_hbm.at[pl.ds(rest, steps - HALF)], sems.at[0]
    )
    if chunks == 1:
        first.start()
    cells = halo_ref[...].astype(jnp.float32)
    for i, part in enumerate((cells, turned(cells))):
        wide[i, :rows, :] = part
        wide[i, rows:, :] = jnp.zeros((8, HALF), jnp.float32)
    for f in range(freqs):
        at = f * modes
        inputs = jnp.concatenate([wide[i, at : at + 8, :] for i in range(2)], axis=1).astype(jnp.bfloat16)
        taps = jnp.concatenate(
            [
                bands[f // each][f % each, :, pl.ds(pl.multiple_of(reach + i * WINDOW, HALF), HALF)]
                for i in range(2)
            ],
            axis=1,
        )
        filtered = lax.dot_general(inputs, taps, LAST, preferred_element_type=jnp.float32)
        more[at : at + modes, :] = filtered[:modes]
    piece = ((filtered_ref[:, pl.ds(place, HALF)] + more[...]) * gain_ref[...]).astype(jnp.bfloat16)
    width = columns_ref.shape[1] // SPLITS
    copies = [first]
    for i in range(SPLITS):
        span = (slice(None), slice(i * width, (i + 1) * width))
        part = lax.dot_general(piece, columns_ref[span], FIRST, preferred_element_type=jnp.float32)
        target = out_hbm.at[pl.ds(place, HALF), pl.ds(i * width, width)]
        copies.append(pltpu.make_async_copy(edge.at[span], target, sems.at[1 + i]))

        def store(values, span=span, copy=copies[-1]):
            edge[span] = values.astype(jnp.bfloat16)
            copy.start()

        add_over_chunks(chunks, total, span, part, store)

    def finish():
        if chunks > 1:
            first.start()
        for copy in copies:
            copy.wait()

    if chunks == 1:
        finish()
    else:
        pl.when(pl.program_id(0) == chunks - 1)(finish)


def band_field(coeffs, halo, bands, gain, columns):
    rows, steps = coeffs.shape
    dofs = columns.shape[1]
    freqs = sum(part.shape[0] for part in bands)
    chunk = min(CHUNK, freqs)
    chunks = freqs // chunk
    one = chunks == 1
    bands = bands if one else [jnp.concatenate(bands)]
    parts = len(bands)
    held = rows // chunks
    grid = () if one else (chunks,)
    made = pltpu.VMEM if one else jax.ShapeDtypeStruct

    def rows_of(width):
        return WHOLE if one else pl.BlockSpec((held, width), lambda i: (i, 0))

    taps = [WHOLE if one else pl.BlockSpec((chunk, HALF, 2 * WINDOW), lambda i: (i, 0, 0))] * parts
    params = pltpu.CompilerParams(vmem_limit_bytes=24 << 20)
    filtered, field = pl.pallas_call(
        functools.partial(own_kernel, chunks, parts),
        grid=grid,
        out_shape=[made((rows, steps), jnp.float32), made((steps, dofs), jnp.bfloat16)],
        in_specs=[rows_of(steps), *taps, rows_of(HALF), rows_of(dofs)],
        out_specs=[rows_of(steps), WHOLE],
        scratch_shapes=[
            pltpu.VMEM((2, held + 8, steps + 2 * HALF), jnp.float32),
            pltpu.VMEM((8 if one else steps, dofs), jnp.float32),
        ],
        compiler_params=params,
        cost_estimate=pl.CostEstimate(
            flops=2 * rows * dofs * steps, bytes_accessed=2 * steps * dofs, transcendentals=0
        ),
        name="own_field",
    )(coeffs, *bands, gain, columns)
    return pl.pallas_call(
        functools.partial(edge_kernel, chunks, parts),
        grid=grid,
        out_shape=jax.ShapeDtypeStruct((steps, dofs), jnp.bfloat16),
        in_specs=[rows_of(HALF), rows_of(steps), *taps, rows_of(HALF), rows_of(dofs), WHOLE],
        out_specs=pl.BlockSpec(memory_space=pl.ANY),
        scratch_shapes=[
            pltpu.VMEM((2, held + 8, HALF), jnp.float32),
            pltpu.VMEM((held, HALF), jnp.float32),
            pltpu.VMEM((HALF, dofs), jnp.bfloat16),
            pltpu.VMEM((8 if one else HALF, dofs), jnp.float32),
            pltpu.SemaphoreType.DMA((1 + SPLITS,)),
        ],
        compiler_params=params,
        cost_estimate=pl.CostEstimate(
            flops=2 * rows * dofs * HALF, bytes_accessed=2 * steps * dofs, transcendentals=0
        ),
        name="edge_field",
    )(halo, filtered, *bands, gain, columns, field)


def message_scale(dofs, all_dofs):
    snapshot, column = 6.0, 0.0625 * math.sqrt(8192 / all_dofs)
    return 2.0 ** math.floor(math.log2(65504 / (dofs * snapshot * column)))


def received(message, masks, swap):
    count, cores = lax.axis_size("space"), lax.axis_size("tm")
    others = []
    for mask in masks:
        mask = mask if isinstance(mask, tuple) else (mask, mask)
        pairs = [
            (place * cores + core, (place ^ mask[place >> 1 & 1]) * cores + (core ^ swap))
            for place in range(count)
            for core in range(cores)
        ]
        others.append(lax.ppermute(message, ("space", "tm"), pairs))
    return others


def exchanged(values, masks, scale, swap, ready=None):
    message = (values * scale).astype(jnp.float16)
    if ready is not None:
        message, ready = lax.optimization_barrier((message, ready))
    more = sum(other.astype(jnp.float32) for other in received(message, masks, swap)) * (1 / scale)
    values = more if swap else values + more
    return values if ready is None else (values, ready)


def per_device(snapshots, mode_columns, filter_taps, mode_gain):
    columns = mode_columns.T
    devices = lax.axis_size("space")
    dofs = columns.shape[1]
    coeffs = coefficients(columns, snapshots)
    coeffs = exchanged(coeffs, ((0, 4), (4, 0)), message_scale(dofs, dofs * devices), 1)
    gain = jnp.broadcast_to(mode_gain[:, None], (mode_gain.shape[0], HALF))
    taps, gain = lax.optimization_barrier((padded_taps(filter_taps), gain))
    bands = band_matrices(taps)
    apart = 8
    while apart < devices:
        coeffs = exchanged(coeffs, (apart,), message_scale(dofs * apart // 4, dofs * devices), 0)
        apart *= 2
    coeffs, bands = exchanged(coeffs, (0, 1, 2, 3), message_scale(dofs * devices // 4, dofs * devices), 1, bands)
    edge = jnp.where(lax.axis_index("tm") == 0, coeffs[:, -HALF:], coeffs[:, :HALF])
    halo = lax.ppermute(edge.astype(jnp.bfloat16), "tm", [(0, 1), (1, 0)])
    return band_field(coeffs, halo, [bands], gain, columns)


def solution(mesh):
    placed = (P(("group", "tm"), "space"), P("space", "group"), P(), P("group"))
    return jax.shard_map(
        per_device,
        mesh=mesh,
        in_specs=placed,
        out_specs=P(("group", "tm"), "space"),
        check_vma=False,
    )
```

```python
import functools
import math

import jax
import jax.numpy as jnp
from jax import lax
from jax.experimental import pallas as pl
from jax.experimental.pallas import tpu as pltpu
from jax.sharding import PartitionSpec as P

HALF = 128
WINDOW = 3 * HALF
CHUNK = 8
SPLITS = 4
LAST = (((1,), (1,)), ((), ()))
FIRST = (((0,), (0,)), ((), ()))
WHOLE = pl.BlockSpec(memory_space=pltpu.VMEM)


def coefficient_kernel(columns_hbm, snapshots_hbm, out_ref, columns, snapshots, sems):
    width = snapshots.shape[1] // SPLITS
    head = pltpu.make_async_copy(columns_hbm, columns, sems.at[SPLITS])
    head.start()
    copies = []
    for i in range(SPLITS):
        span = pl.ds(i * width, width)
        copies.append(pltpu.make_async_copy(snapshots_hbm.at[:, span], snapshots.at[:, span], sems.at[i]))
        copies[-1].start()
    head.wait()
    total = None
    for i, copy in enumerate(copies):
        copy.wait()
        span = slice(i * width, (i + 1) * width)
        part = lax.dot_general(columns[:, span], snapshots[:, span], LAST, preferred_element_type=jnp.float32)
        total = part if total is None else total + part
    out_ref[...] = total


def coefficients(columns, snapshots):
    rows, dofs = columns.shape
    steps = snapshots.shape[0]
    return pl.pallas_call(
        coefficient_kernel,
        out_shape=pltpu.VMEM((rows, steps), jnp.float32),
        in_specs=[pl.BlockSpec(memory_space=pltpu.HBM)] * 2,
        out_specs=WHOLE,
        scratch_shapes=[
            pltpu.VMEM((rows, dofs), jnp.bfloat16),
            pltpu.VMEM((steps, dofs), jnp.bfloat16),
            pltpu.SemaphoreType.DMA((SPLITS + 1,)),
        ],
        compiler_params=pltpu.CompilerParams(vmem_limit_bytes=16 << 20),
        cost_estimate=pl.CostEstimate(
            flops=2 * rows * dofs * steps, bytes_accessed=2 * steps * dofs, transcendentals=0
        ),
        name="coefficients",
    )(pltpu.with_memory_space_constraint(columns, pltpu.HBM), pltpu.with_memory_space_constraint(snapshots, pltpu.HBM))


def band_kernel(taps_ref, out_ref):
    for f in range(out_ref.shape[0]):
        for part in range(2):
            row = taps_ref[2 * f + part : 2 * f + part + 1, :]
            square = jnp.broadcast_to(row, (HALF, WINDOW))
            out_ref[f, :, part * WINDOW : (part + 1) * WINDOW] = pltpu.roll(
                square, 0, 1, stride=1, stride_axis=0
            ).astype(jnp.bfloat16)


def padded_taps(filter_taps):
    freqs, parts, taps = filter_taps.shape
    rows = filter_taps.astype(jnp.float32).reshape(freqs * parts, taps)
    return jnp.pad(rows, ((0, 0), (0, WINDOW - taps)))


def band_matrices(taps):
    freqs = taps.shape[0] // 2
    chunk = min(CHUNK, freqs)
    one = freqs == chunk
    shape = (freqs, HALF, 2 * WINDOW)
    return pl.pallas_call(
        band_kernel,
        grid=() if one else (freqs // chunk,),
        out_shape=pltpu.VMEM(shape, jnp.bfloat16) if one else jax.ShapeDtypeStruct(shape, jnp.bfloat16),
        in_specs=[WHOLE if one else pl.BlockSpec((2 * chunk, WINDOW), lambda i: (i, 0))],
        out_specs=WHOLE if one else pl.BlockSpec((chunk, HALF, 2 * WINDOW), lambda i: (i, 0, 0)),
        compiler_params=pltpu.CompilerParams(vmem_limit_bytes=16 << 20),
        cost_estimate=pl.CostEstimate(
            flops=freqs * HALF * WINDOW * 40, bytes_accessed=freqs * HALF * WINDOW * 4, transcendentals=0
        ),
        name="band_matrices",
    )(taps)


def turned(cells):
    cosine = lax.broadcasted_iota(jnp.int32, cells.shape, 0) % 2 == 0
    return jnp.where(cosine, -pltpu.roll(cells, cells.shape[0] - 1, 0), pltpu.roll(cells, 1, 0))


def add_over_chunks(chunks, total, span, part, store):
    if chunks == 1:
        store(part)
        return
    step = pl.program_id(0)
    total[span] = jnp.where(step == 0, part, total[span] + part)

    @pl.when(step == chunks - 1)
    def _():
        store(total[span])


def places(steps):
    after = lax.axis_index("tm") == 0
    rest = pl.multiple_of(jnp.where(after, 0, HALF), HALF)
    return rest, pl.multiple_of(jnp.where(after, steps - HALF, 0), HALF)


def own_kernel(chunks, parts, coeffs_ref, *refs):
    bands, (gain_ref, columns_ref, filtered_ref, field_ref, wide, total) = refs[:parts], refs[parts:]
    rows, steps = coeffs_ref.shape
    blocks = steps // HALF
    each = bands[0].shape[0]
    freqs = parts * each
    modes = rows // freqs
    half = HALF // 2
    cells = coeffs_ref[...].astype(jnp.bfloat16).astype(jnp.float32)
    none = jnp.zeros((rows, HALF), jnp.float32)
    cells = jnp.concatenate([none, cells, none], axis=1)
    extent = cells.shape[1]
    for i, part in enumerate((cells, turned(cells))):
        wide[i, :rows, :] = part
        wide[2 + i, :rows, :] = pltpu.roll(part, extent - half, 1)
    wide[:, rows:, :] = jnp.zeros((4, 8, extent), jnp.float32)
    for f in range(freqs):
        at = f * modes
        inputs = jnp.concatenate(
            [
                jnp.concatenate(
                    [wide[2 * late + i, at : at + 8, b * HALF : b * HALF + WINDOW] for i in range(2)], axis=1
                )
                for b in range(blocks)
                for late in range(2)
            ],
            axis=0,
        ).astype(jnp.bfloat16)
        band = bands[f // each][f % each, :half, :]
        filtered = lax.dot_general(inputs, band, LAST, preferred_element_type=jnp.float32)
        for b in range(blocks):
            pair = [filtered[8 * k : 8 * k + modes] for k in (2 * b, 2 * b + 1)]
            filtered_ref[at : at + modes, b * HALF : (b + 1) * HALF] = jnp.concatenate(pair, axis=1)
    columns = columns_ref[...]
    rest, _ = places(steps)
    alone = steps - HALF
    span = pl.ds(rest, alone)
    gain = jnp.concatenate([gain_ref[...]] * (blocks - 1), axis=1)
    piece = (filtered_ref[:, span] * gain).astype(jnp.bfloat16)
    width = columns.shape[1] // SPLITS
    for i in range(SPLITS):
        place = (span, slice(i * width, (i + 1) * width))
        part = lax.dot_general(piece, columns[:, place[1]], FIRST, preferred_element_type=jnp.float32)

        def store(values, place=place):
            field_ref[place] = values.astype(jnp.bfloat16)

        add_over_chunks(chunks, total, place, part, store)


def edge_kernel(chunks, parts, halo_ref, filtered_ref, *refs):
    bands, refs = refs[:parts], refs[parts:]
    gain_ref, columns_ref, field_ref, out_hbm, wide, more, edge, total, sems = refs
    rows, steps = filtered_ref.shape
    each = bands[0].shape[0]
    freqs = parts * each
    modes = rows // freqs
    rest, place = places(steps)
    reach = pl.multiple_of(jnp.where(rest == 0, WINDOW - HALF, 0), HALF)
    first = pltpu.make_async_copy(
        field_ref.at[pl.ds(rest, steps - HALF)], out_hbm.at[pl.ds(rest, steps - HALF)], sems.at[0]
    )
    if chunks == 1:
        first.start()
    cells = halo_ref[...].astype(jnp.float32)
    for i, part in enumerate((cells, turned(cells))):
        wide[i, :rows, :] = part
        wide[i, rows:, :] = jnp.zeros((8, HALF), jnp.float32)
    for f in range(freqs):
        at = f * modes
        inputs = jnp.concatenate([wide[i, at : at + 8, :] for i in range(2)], axis=1).astype(jnp.bfloat16)
        taps = jnp.concatenate(
            [
                bands[f // each][f % each, :, pl.ds(pl.multiple_of(reach + i * WINDOW, HALF), HALF)]
                for i in range(2)
            ],
            axis=1,
        )
        filtered = lax.dot_general(inputs, taps, LAST, preferred_element_type=jnp.float32)
        more[at : at + modes, :] = filtered[:modes]
    piece = ((filtered_ref[:, pl.ds(place, HALF)] + more[...]) * gain_ref[...]).astype(jnp.bfloat16)
    width = columns_ref.shape[1] // SPLITS
    copies = [first]
    for i in range(SPLITS):
        span = (slice(None), slice(i * width, (i + 1) * width))
        part = lax.dot_general(piece, columns_ref[span], FIRST, preferred_element_type=jnp.float32)
        target = out_hbm.at[pl.ds(place, HALF), pl.ds(i * width, width)]
        copies.append(pltpu.make_async_copy(edge.at[span], target, sems.at[1 + i]))

        def store(values, span=span, copy=copies[-1]):
            edge[span] = values.astype(jnp.bfloat16)
            copy.start()

        add_over_chunks(chunks, total, span, part, store)

    def finish():
        if chunks > 1:
            first.start()
        for copy in copies:
            copy.wait()

    if chunks == 1:
        finish()
    else:
        pl.when(pl.program_id(0) == chunks - 1)(finish)


def band_field(coeffs, halo, bands, gain, columns):
    rows, steps = coeffs.shape
    dofs = columns.shape[1]
    freqs = sum(part.shape[0] for part in bands)
    chunk = min(CHUNK, freqs)
    chunks = freqs // chunk
    one = chunks == 1
    bands = bands if one else [jnp.concatenate(bands)]
    parts = len(bands)
    held = rows // chunks
    grid = () if one else (chunks,)
    made = pltpu.VMEM if one else jax.ShapeDtypeStruct

    def rows_of(width):
        return WHOLE if one else pl.BlockSpec((held, width), lambda i: (i, 0))

    taps = [WHOLE if one else pl.BlockSpec((chunk, HALF, 2 * WINDOW), lambda i: (i, 0, 0))] * parts
    params = pltpu.CompilerParams(vmem_limit_bytes=24 << 20)
    filtered, field = pl.pallas_call(
        functools.partial(own_kernel, chunks, parts),
        grid=grid,
        out_shape=[made((rows, steps), jnp.float32), made((steps, dofs), jnp.bfloat16)],
        in_specs=[rows_of(steps), *taps, rows_of(HALF), rows_of(dofs)],
        out_specs=[rows_of(steps), WHOLE],
        scratch_shapes=[
            pltpu.VMEM((4, held + 8, steps + 2 * HALF), jnp.float32),
            pltpu.VMEM((8 if one else steps, dofs), jnp.float32),
        ],
        compiler_params=params,
        cost_estimate=pl.CostEstimate(
            flops=2 * rows * dofs * steps, bytes_accessed=2 * steps * dofs, transcendentals=0
        ),
        name="own_field",
    )(coeffs, *bands, gain, columns)
    return pl.pallas_call(
        functools.partial(edge_kernel, chunks, parts),
        grid=grid,
        out_shape=jax.ShapeDtypeStruct((steps, dofs), jnp.bfloat16),
        in_specs=[rows_of(HALF), rows_of(steps), *taps, rows_of(HALF), rows_of(dofs), WHOLE],
        out_specs=pl.BlockSpec(memory_space=pl.ANY),
        scratch_shapes=[
            pltpu.VMEM((2, held + 8, HALF), jnp.float32),
            pltpu.VMEM((held, HALF), jnp.float32),
            pltpu.VMEM((HALF, dofs), jnp.bfloat16),
            pltpu.VMEM((8 if one else HALF, dofs), jnp.float32),
            pltpu.SemaphoreType.DMA((1 + SPLITS,)),
        ],
        compiler_params=params,
        cost_estimate=pl.CostEstimate(
            flops=2 * rows * dofs * HALF, bytes_accessed=2 * steps * dofs, transcendentals=0
        ),
        name="edge_field",
    )(halo, filtered, *bands, gain, columns, field)


def message_scale(dofs, all_dofs):
    snapshot, column = 6.0, 0.0625 * math.sqrt(8192 / all_dofs)
    return 2.0 ** math.floor(math.log2(65504 / (dofs * snapshot * column)))


def received(message, masks, swap):
    count, cores = lax.axis_size("space"), lax.axis_size("tm")
    others = []
    for mask in masks:
        mask = mask if isinstance(mask, tuple) else (mask, mask)
        pairs = [
            (place * cores + core, (place ^ mask[place >> 1 & 1]) * cores + (core ^ swap))
            for place in range(count)
            for core in range(cores)
        ]
        others.append(lax.ppermute(message, ("space", "tm"), pairs))
    return others


def exchanged(values, masks, scale, swap, ready=None):
    message = (values * scale).astype(jnp.float16)
    if ready is not None:
        message, ready = lax.optimization_barrier((message, ready))
    others = received(message, masks, swap)
    more = sum(other.astype(jnp.float32) for other in others) * (1 / scale)
    if ready is None:
        return more if swap else values + more
    low = lax.axis_index("tm") == 0
    ends = [jnp.where(low, other[:, -HALF:], other[:, :HALF]).astype(jnp.float32) for other in others]
    edge = (sum(ends) * (1 / scale)).astype(jnp.bfloat16)
    return more, edge, ready


def per_device(snapshots, mode_columns, filter_taps, mode_gain):
    columns = mode_columns.T
    devices = lax.axis_size("space")
    dofs = columns.shape[1]
    coeffs = coefficients(columns, snapshots)
    coeffs = exchanged(coeffs, ((0, 4), (4, 0)), message_scale(dofs, dofs * devices), 1)
    gain = jnp.broadcast_to(mode_gain[:, None], (mode_gain.shape[0], HALF))
    taps, gain = lax.optimization_barrier((padded_taps(filter_taps), gain))
    bands = band_matrices(taps)
    apart = 8
    while apart < devices:
        coeffs = exchanged(coeffs, (apart,), message_scale(dofs * apart // 4, dofs * devices), 0)
        apart *= 2
    coeffs, edge, bands = exchanged(coeffs, (0, 1, 2, 3), message_scale(dofs * devices // 4, dofs * devices), 1, bands)
    halo = lax.ppermute(edge, "tm", [(0, 1), (1, 0)])
    return band_field(coeffs, halo, [bands], gain, columns)


def solution(mesh):
    placed = (P(("group", "tm"), "space"), P("space", "group"), P(), P("group"))
    return jax.shard_map(
        per_device,
        mesh=mesh,
        in_specs=placed,
        out_specs=P(("group", "tm"), "space"),
        check_vma=False,
    )
```
